256 devices in a mesh: ka: 64 (over x, z_lo, y), aux: 4 (over z_hi, core).
Axes of the slice: x: 4, y: 4, z: 8 (z_hi: 2, z_lo: 4; z = z_hi * 4 + z_lo), core: 2. Of those that a mesh axis runs over, the one named last changes fastest.
Arguments:
- lambda_blocks: bfloat16 [64, 8, 16, 64, 64], P('ka', None, 'aux'), may hold values from -6 to 6
- left_tiles: bfloat16 [64, 2, 256, 64, 64], P('ka', None, 'aux'), may hold values from -0.1875 to 0.1875
- right_tiles: bfloat16 [64, 2, 256, 64, 64], P('ka', None, 'aux'), may hold values from -0.1875 to 0.1875
Outputs:
- ladder: float32 [64, 8, 16, 64, 64], P('ka', None, 'aux')
The draws below stay inside these ranges and needn't reach their ends.
All inputs are finite; a program needn't handle non-finite values.
Results may differ from the reference program's by a relative error of at most 0.0029.
Values may be sent and summed in bfloat16 or wider, within the bound.
No kernel may reach another device: no remote copies, remote signals or barrier semaphores. Data moves between devices by JAX's collectives and lax.ppermute only.
A program may use at most 64 MiB of HBM per device.

```python
import jax
import jax.numpy as jnp
from jax import lax

V = 64
O = 16
OI = 8
NAUX = 256
NK = 64
GROUPS = 4
FAR = 16


def shard_levels(own_key, shape, split, smallest, top_value):
    level, own = 1.0, jax.random.fold_in(own_key, 6)
    for position, blocks in split:
        draws = jnp.exp(jax.random.uniform(jax.random.fold_in(own, position), (blocks,), jnp.float32, smallest / len(split), top_value / len(split)))
        level = level * jnp.repeat(draws, shape[position] // blocks).reshape([-1 if axis == position else 1 for axis in range(len(shape))])
    return level


def normal_values(key, extent, width, bound, shards=(), held_as=jnp.bfloat16):
    array = width * jax.random.normal(key, extent, jnp.float32)
    if shards:
        array = array * shard_levels(key, extent, shards, -0.22, 0.18)
    return jnp.clip(array, -bound, bound).astype(held_as)


def setup_inputs(seed: int = 0) -> dict:
    key_list = jax.random.split(jax.random.key(seed), 4)
    lambda_blocks = normal_values(key_list[0], (NK, OI, O, V, V), 1.0, 6.0, ((0, 64), (2, 4)))
    left_tiles = normal_values(key_list[1], (NK, 2, NAUX, V, V), (V * V // 4) ** -0.5, 0.1875, ((0, 64), (2, 4)))
    right_tiles = normal_values(key_list[2], (NK, 2, NAUX, V, V), (V * V // 4) ** -0.5, 0.1875, ((0, 64), (2, 4)))
    return {"lambda_blocks": lambda_blocks, "left_tiles": left_tiles, "right_tiles": right_tiles}


def one_point(args):
    kpoint, left, right, blocks_near, blocks_far = args
    total = jnp.zeros((OI, O, V, V), jnp.float32)
    for offset, partner in ((0, blocks_near), (1, blocks_far)):
        left_g = left[offset].astype(jnp.float32).reshape(GROUPS, NAUX // GROUPS, V, V)
        right_g = right[offset].astype(jnp.float32).reshape(GROUPS, NAUX // GROUPS, V, V)
        vvvv = jnp.zeros((V, V, V, V), jnp.float32)
        for group in range(GROUPS):
            part = jnp.einsum("lac,lbd->cdab", left_g[group], right_g[group], precision=lax.Precision.HIGHEST)
            vvvv = vvvv + part.astype(jnp.bfloat16).astype(jnp.float32)
        total = total + jnp.einsum("ijcd,cdab->ijab", partner.astype(jnp.float32), vvvv, precision=lax.Precision.HIGHEST)
    return total


def reference(lambda_blocks, left_tiles, right_tiles):
    near = jnp.roll(lambda_blocks, -1, axis=0)
    far = jnp.roll(lambda_blocks, -FAR, axis=0)
    kpoints = jnp.arange(NK, dtype=jnp.int32)
    return lax.map(one_point, (kpoints, left_tiles, right_tiles, near, far))
```

```python
import functools

import jax
import jax.numpy as jnp
from jax import lax
from jax.experimental import pallas as pl
from jax.experimental.pallas import tpu as pltpu
from jax.sharding import PartitionSpec as P

BF16 = jnp.bfloat16
F32 = jnp.float32
VMEM = pl.BlockSpec(memory_space=pltpu.VMEM)
SMEM = pl.BlockSpec(memory_space=pltpu.SMEM)
ANY = pl.BlockSpec(memory_space=pl.ANY)
MIB = 2**20


def params(mib, **kw):
    return pltpu.CompilerParams(vmem_limit_bytes=mib * MIB, **kw)


def spread(src, dst, held, count, swap, unroll):
    def put(n, _):
        x = src[n].T if swap else src[n]
        rows = pl.ds(pl.multiple_of(n * 32, 32), 32)
        held[rows, :] = jnp.concatenate([x[:32], x[32:]], axis=1).astype(F32)
        return 0

    lax.fori_loop(0, count, put, 0, unroll=unroll)
    for t in range(32):
        dst[:, t * 128 : (t + 1) * 128] = held[pl.ds(t, count, stride=32), :].astype(BF16)


def in_hbm(x):
    return pltpu.with_memory_space_constraint(x, pltpu.HBM)


def in_vmem(x):
    return pltpu.with_memory_space_constraint(x, pltpu.VMEM)


def cost(flops, mib):
    return pl.CostEstimate(flops=flops, bytes_accessed=int(mib * MIB), transcendentals=0)


def lambda_kernel(lam, out, held):
    spread(lam, out, held, lam.shape[0], True, 32)


def flat_lambda(lam):
    n = lam.shape[0]
    return pl.pallas_call(
        lambda_kernel,
        grid=(1,),
        out_shape=jax.ShapeDtypeStruct((n, 4096), BF16),
        in_specs=[pl.BlockSpec((n, 64, 64), lambda i: (0, 0, 0))],
        out_specs=pl.BlockSpec((n, 4096), lambda i: (0, 0)),
        scratch_shapes=[pltpu.VMEM((n * 32, 128), F32)],
        compiler_params=params(8),
        cost_estimate=cost(0, 6),
        name="flat_lambda",
    )(in_hbm(lam))


def factor_kernel(left, right, left_out, right_out, held_l, held_r):
    spread(left.at[0], left_out, held_l, 32, False, 32)
    spread(right.at[0], right_out, held_r, 32, True, 32)


def flat_factors(left, right, s):
    block = pl.BlockSpec((1, 32, 64, 64), lambda i: (s, i, 0, 0))
    flat = pl.BlockSpec((32, 4096), lambda i: (i, 0))
    shape = jax.ShapeDtypeStruct((64, 4096), BF16)
    return pl.pallas_call(
        factor_kernel,
        grid=(2,),
        out_shape=[shape, shape],
        in_specs=[block, block],
        out_specs=[flat, flat],
        scratch_shapes=[pltpu.VMEM((32 * 32, 128), F32)] * 2,
        compiler_params=params(8),
        cost_estimate=cost(0, 12),
        name="flat_factors",
    )(in_hbm(left), in_hbm(right))


TS = 4
HALF = 16


def build_kernel(first, core, left_mine, left_other, right_mine, right_other, w, x, s):
    half = core[0]
    for ap in range(16):
        at = pl.ds(pl.multiple_of((half * 16 + ap) * 128, 128), 128)
        v = jnp.concatenate([left_mine[:, at], left_other[:, at]], axis=0).T
        x[ap * 64 : (ap + 1) * 64, :] = jnp.concatenate([v[:64], v[64:]], axis=1)
    low = lax.broadcasted_iota(jnp.int32, (128, 128), 1) < 64
    zero = jnp.zeros((128, 128), BF16)

    def fill(slot, u):
        for i in range(TS):
            t = first + jnp.minimum(u * TS + i, HALF - 1)
            at = pl.ds(pl.multiple_of(t * 128, 128), 128)
            v = jnp.concatenate([right_mine[:, at], right_other[:, at]], axis=0)
            r = jnp.concatenate([v[:, 64:], v[:, :64]], axis=1)
            a, b = i * 256, i * 256 + 128
            s[slot, 0:128, a : a + 128] = jnp.where(low, v, zero)
            s[slot, 0:128, b : b + 128] = jnp.where(low, r, zero)
            s[slot, 128:256, a : a + 128] = jnp.where(low, zero, r)
            s[slot, 128:256, b : b + 128] = jnp.where(low, zero, v)

    def work(u, slot):
        fill(1 - slot, u + 1)
        for m in range(8):
            got = jnp.dot(x[m * 128 : (m + 1) * 128, :], s[slot], preferred_element_type=F32).astype(BF16)
            for i in range(TS * 2):
                at = pl.ds(pl.multiple_of((u * TS * 2 + i) * 64, 64), 64)
                for p in range(2):
                    w[at, (m * 2 + p) * 128 : (m * 2 + p + 1) * 128] = got[
                        p * 64 : (p + 1) * 64, i * 128 : (i + 1) * 128
                    ]

    def pair(v, _):
        work(v * 2, 0)
        work(v * 2 + 1, 1)
        return 0

    fill(0, 0)
    lax.fori_loop(0, HALF // TS // 2, pair, 0)


def build(first, core, left_mine, left_other, right_mine, right_other):
    return pl.pallas_call(
        functools.partial(build_kernel, first),
        out_shape=pltpu.VMEM((HALF * 128, 2048), BF16),
        in_specs=[SMEM] + [VMEM] * 4,
        out_specs=VMEM,
        scratch_shapes=[pltpu.VMEM((1024, 256), BF16), pltpu.VMEM((2, 256, 256 * TS), BF16)],
        compiler_params=params(6),
        cost_estimate=cost(2 * 1024 * 256 * 4096, 9),
        name="build_w",
    )(core, left_mine, left_other, right_mine, right_other)


def contract_kernel(chunk, *refs):
    pieces, ws, outs, (lhs, sems) = refs[:8], refs[8:12], refs[12:16], refs[16:]
    copies = []
    for p, piece in enumerate(pieces):
        rows = pl.ds(p % 4 * 32, 32)
        copies.append(pltpu.make_async_copy(piece, lhs.at[p // 4, rows], sems.at[p]))
    for c in copies:
        c.start()
    for c in copies:
        c.wait()
    own, core, zed, diag = outs
    width = 512
    for n in range(COLS // width):
        at = slice(n * width, (n + 1) * width)
        src = slice(chunk * COLS + n * width, chunk * COLS + (n + 1) * width)
        got = jnp.zeros((128, width), F32)
        for i, w in enumerate(ws):
            k = HALF * 128 * (i % 2)
            got += jnp.dot(lhs[i // 2, :, k : k + HALF * 128], w[:, src], preferred_element_type=F32)
        own[:, at] = got[0:32]
        core[:, at] = got[32:64]
        zed[:, at] = got[64:96].astype(BF16)
        diag[:, at] = got[96:128].astype(BF16)


COLS = 1024


def contract(chunk, pieces, ws):
    return pl.pallas_call(
        functools.partial(contract_kernel, chunk),
        out_shape=[jax.ShapeDtypeStruct((32, COLS), t) for t in (F32, F32, BF16, BF16)],
        in_specs=[ANY] * 8 + [VMEM] * 4,
        out_specs=[VMEM] * 4,
        scratch_shapes=[pltpu.VMEM((2, 128, 4096), BF16), pltpu.SemaphoreType.DMA((8,))],
        compiler_params=params(8),
        cost_estimate=cost(4 * 128 * 4096 * COLS, 12),
        name="contract",
    )(*pieces, *(in_vmem(w) for w in ws))


def finish_kernel(core, *refs):
    parts, out, held = refs[:-2], refs[-2], refs[-1]
    half = core[0]
    per = COLS // 128
    for ap in range(16):
        own, zed, other, diag = parts[ap // per * 4 : ap // per * 4 + 4]
        at = slice(ap % per * 128, (ap % per + 1) * 128)
        held[pl.ds(half * 16 + ap, 32, stride=32), :] = own[:, at] + zed[:, at].astype(F32)
        held[pl.ds((1 - half) * 16 + ap, 32, stride=32), :] = other[:, at] + diag[:, at].astype(F32)

    def put(n, _):
        x = held[pl.ds(pl.multiple_of(n * 32, 32), 32), :]
        out[n, 0:32, :] = x[:, :64]
        out[n, 32:64, :] = x[:, 64:]
        return 0

    lax.fori_loop(0, 32, put, 0, unroll=16)


def finish(core, parts):
    return pl.pallas_call(
        finish_kernel,
        out_shape=jax.ShapeDtypeStruct((32, 64, 64), F32),
        in_specs=[SMEM] + [VMEM] * len(parts),
        out_specs=VMEM,
        scratch_shapes=[pltpu.VMEM((1024, 128), F32)],
        compiler_params=params(8),
        cost_estimate=cost(0, 6),
        name="finish",
    )(core, *parts)


AXES = ("ka", "aux")


def moved(x, points, parts, source):
    route = []
    for k in range(points):
        for a in range(parts):
            k2, a2 = source(k, a)
            route.append((k2 * parts + a2, k * parts + a))
    return lax.ppermute(x, AXES, route)


def body(lambda_blocks, left_tiles, right_tiles):
    points, parts = lax.axis_size("ka"), lax.axis_size("aux")
    go = lambda x, source: moved(x, points, parts, source)
    near = lambda x: go(x, lambda k, a: ((k + 1) % points, a))
    far = lambda x: go(x, lambda k, a: ((k + points // 4) % points, a))
    zed = lambda x: go(x, lambda k, a: (k, a ^ 2))
    core = lambda x: go(x, lambda k, a: (k, a ^ 1))
    diag = lambda x: go(x, lambda k, a: (k, a ^ 3))
    which = (lax.axis_index("aux") % 2).astype(jnp.int32).reshape(1)

    lam = flat_lambda(lambda_blocks.reshape(32, 64, 64))
    lam_z = zed(lam)
    near_own, far_own = near(lam), far(lam)
    ws = []
    for s in range(2):
        left, right = flat_factors(left_tiles[0], right_tiles[0], s)
        left_other, right_other = core(left), core(right)
        ws += [build(first, which, left, left_other, right, right_other) for first in (0, HALF)]
    near_z, far_z = near(lam_z), far(lam_z)
    pieces = [near_own, core(near_own), near_z, core(near_z), far_own, core(far_own), far_z, core(far_z)]
    sums = []
    for chunk in range(2048 // COLS):
        p_own, p_core, p_zed, p_diag = contract(chunk, pieces, ws)
        sums += [p_own, zed(p_zed), core(p_core), diag(p_diag)]
    out = finish(which, sums)
    return out.reshape(lambda_blocks.shape)


def solution(mesh):
    placed = P("ka", None, "aux", None, None)
    return jax.shard_map(body, mesh=mesh, in_specs=(placed,) * 3, out_specs=placed, check_vma=False)
```

```python
import functools

import jax
import jax.numpy as jnp
from jax import lax
from jax.experimental import pallas as pl
from jax.experimental.pallas import tpu as pltpu
from jax.sharding import PartitionSpec as P

BF16 = jnp.bfloat16
F32 = jnp.float32
VMEM = pl.BlockSpec(memory_space=pltpu.VMEM)
SMEM = pl.BlockSpec(memory_space=pltpu.SMEM)
ANY = pl.BlockSpec(memory_space=pl.ANY)
MIB = 2**20


def params(mib, **kw):
    return pltpu.CompilerParams(vmem_limit_bytes=mib * MIB, **kw)


def spread(src, dst, held, count, swap, unroll):
    def put(n, _):
        x = src[n].T if swap else src[n]
        rows = pl.ds(pl.multiple_of(n * 32, 32), 32)
        held[rows, :] = jnp.concatenate([x[:32], x[32:]], axis=1).astype(F32)
        return 0

    lax.fori_loop(0, count, put, 0, unroll=unroll)
    for ref, first in dst:
        take(ref, held, first, count)


def take(dst, held, first, count):
    for t in range(dst.shape[1] // 128):
        dst[:, t * 128 : (t + 1) * 128] = held[pl.ds(first + t, count, stride=32), :].astype(BF16)


def in_hbm(x):
    return pltpu.with_memory_space_constraint(x, pltpu.HBM)


def in_vmem(x):
    return pltpu.with_memory_space_constraint(x, pltpu.VMEM)


def cost(flops, mib):
    return pl.CostEstimate(flops=flops // 1000, bytes_accessed=int(mib * 1024), transcendentals=0)


def lambda_kernel(lam, out, again, held):
    spread(lam, [(out, 0)], held, lam.shape[0], True, 32)
    again[...] = out[...]


def flat_lambda(lam):
    n = lam.shape[0]
    flat = pl.BlockSpec((n, 4096), lambda i: (0, 0))
    return pl.pallas_call(
        lambda_kernel,
        grid=(1,),
        out_shape=[jax.ShapeDtypeStruct((n, 4096), BF16)] * 2,
        in_specs=[pl.BlockSpec((n, 64, 64), lambda i: (0, 0, 0))],
        out_specs=[flat] * 2,
        scratch_shapes=[pltpu.VMEM((n * 32, 128), F32)],
        compiler_params=params(8),
        cost_estimate=cost(0, 6),
        name="flat_lambda",
    )(in_hbm(lam))


def factor_kernel(core, left, right, done, mine, sent, held_l, held_r):
    half = core[0]
    spread(left.at[0], [(mine, half * 16), (sent.at[:, :2048], (1 - half) * 16)], held_l, 32, False, 32)
    spread(right.at[0], [(sent.at[:, 2048:], 0)], held_r, 32, True, 32)


def flat_factors(core, left, right, s, done):
    block = pl.BlockSpec((1, 32, 64, 64), lambda i: (s, i, 0, 0))
    return pl.pallas_call(
        factor_kernel,
        grid=(2,),
        out_shape=[jax.ShapeDtypeStruct((64, n), BF16) for n in (2048, 6144)],
        in_specs=[SMEM, block, block, ANY],
        out_specs=[pl.BlockSpec((32, n), lambda i: (i, 0)) for n in (2048, 6144)],
        scratch_shapes=[pltpu.VMEM((32 * 32, 128), F32)] * 2,
        compiler_params=params(8),
        cost_estimate=cost(0, 400000),
        name="flat_factors",
    )(core, in_hbm(left), in_hbm(right), done)


TS = 4
HALF = 16


def build_kernel(first, mine, sent, got_here, done, w, x, s):
    for ap in range(16):
        at = slice(ap * 128, (ap + 1) * 128)
        v = jnp.concatenate([mine[:, at], got_here[:, at]], axis=0).T
        x[ap * 64 : (ap + 1) * 64, :] = jnp.concatenate([v[:64], v[64:]], axis=1)
    low = lax.broadcasted_iota(jnp.int32, (128, 128), 1) < 64
    zero = jnp.zeros((128, 128), BF16)

    def fill(slot, u):
        for i in range(TS):
            t = first + jnp.minimum(u * TS + i, HALF - 1)
            at = pl.ds(pl.multiple_of(2048 + t * 128, 128), 128)
            v = jnp.concatenate([sent[:, at], got_here[:, at]], axis=0)
            r = jnp.concatenate([v[:, 64:], v[:, :64]], axis=1)
            a, b = i * 256, i * 256 + 128
            s[slot, 0:128, a : a + 128] = jnp.where(low, v, zero)
            s[slot, 0:128, b : b + 128] = jnp.where(low, r, zero)
            s[slot, 128:256, a : a + 128] = jnp.where(low, zero, r)
            s[slot, 128:256, b : b + 128] = jnp.where(low, zero, v)

    def work(u, slot):
        fill(1 - slot, u + 1)
        for m in range(8):
            got = jnp.dot(x[m * 128 : (m + 1) * 128, :], s[slot], preferred_element_type=F32).astype(BF16)
            for i in range(TS * 2):
                at = pl.ds(pl.multiple_of((u * TS * 2 + i) * 64, 64), 64)
                for p in range(2):
                    w[at, (m * 2 + p) * 128 : (m * 2 + p + 1) * 128] = got[
                        p * 64 : (p + 1) * 64, i * 128 : (i + 1) * 128
                    ]

    def pair(v, _):
        work(v * 2, 0)
        work(v * 2 + 1, 1)
        return 0

    fill(0, 0)
    lax.fori_loop(0, HALF // TS // 2, pair, 0)


def build(first, mine, sent, got, done, weight=1):
    return pl.pallas_call(
        functools.partial(build_kernel, first),
        out_shape=pltpu.VMEM((HALF * 128, 2048), BF16),
        in_specs=[VMEM] * 3 + [ANY],
        out_specs=VMEM,
        scratch_shapes=[pltpu.VMEM((1024, 256), BF16), pltpu.VMEM((2, 256, 256 * TS), BF16)],
        compiler_params=params(6),
        cost_estimate=cost(2 * 1024 * 256 * 4096 * weight, 9 * weight),
        name="build_w",
    )(mine, sent, got, done)


def contract_kernel(last, first, *refs):
    n_out = 4 if last else 1
    pieces, ws, so_far, outs, (lhs, sems) = refs[:4], refs[4:6], refs[6:-2 - n_out], refs[-2 - n_out : -2], refs[-2:]
    copies = []
    for p, piece in enumerate(pieces):
        copies.append(pltpu.make_async_copy(piece, lhs.at[pl.ds(p * 32, 32)], sems.at[p]))
    for c in copies:
        c.start()
    for c in copies:
        c.wait()
    width = 512
    deep = HALF * 128
    for n in range(outs[0].shape[1] // width):
        at = slice(n * width, (n + 1) * width)
        src = slice(first + n * width, first + (n + 1) * width)
        got = jnp.dot(lhs[:, :deep], ws[0][:, src], preferred_element_type=F32)
        got += jnp.dot(lhs[:, deep:], ws[1][:, src], preferred_element_type=F32)
        if last:
            got += so_far[0][:, src]
            own, core, zed, diag = outs
            own[:, at] = got[0:32]
            core[:, at] = got[32:64]
            zed[:, at] = got[64:96].astype(BF16)
            diag[:, at] = got[96:128].astype(BF16)
        else:
            outs[0][:, at] = got


def contract(pieces, ws, so_far=None, first=0, cols=2048):
    last = so_far is not None
    rows = ((32, F32), (32, F32), (32, BF16), (32, BF16)) if last else ((128, F32),)
    return pl.pallas_call(
        functools.partial(contract_kernel, last, first),
        out_shape=[jax.ShapeDtypeStruct((r, cols), t) for r, t in rows],
        in_specs=[ANY] * 4 + [VMEM] * (2 + last),
        out_specs=[VMEM] * len(rows),
        scratch_shapes=[pltpu.VMEM((128, 4096), BF16), pltpu.SemaphoreType.DMA((4,))],
        compiler_params=params(8),
        cost_estimate=cost(2 * 128 * 4096 * 2048, 12),
        name="contract",
    )(*pieces, *(in_vmem(w) for w in ws), *((so_far,) if last else ()))


def finish_kernel(core, *refs):
    parts, out, held = refs[:-2], refs[-2], refs[-1]
    half = core[0]
    per = 16
    for ap in range(16):
        own, zed, other, diag = parts[ap // per * 4 : ap // per * 4 + 4]
        at = slice(ap % per * 128, (ap % per + 1) * 128)
        held[pl.ds(half * 16 + ap, 32, stride=32), :] = own[:, at] + zed[:, at].astype(F32)
        held[pl.ds((1 - half) * 16 + ap, 32, stride=32), :] = other[:, at] + diag[:, at].astype(F32)

    def put(n, _):
        x = held[pl.ds(pl.multiple_of(n * 32, 32), 32), :]
        out[n, 0:32, :] = x[:, :64]
        out[n, 32:64, :] = x[:, 64:]
        return 0

    lax.fori_loop(0, 32, put, 0, unroll=16)


def finish(core, parts):
    return pl.pallas_call(
        finish_kernel,
        out_shape=jax.ShapeDtypeStruct((32, 64, 64), F32),
        in_specs=[SMEM] + [VMEM] * len(parts),
        out_specs=VMEM,
        scratch_shapes=[pltpu.VMEM((1024, 128), F32)],
        compiler_params=params(8),
        cost_estimate=cost(0, 6),
        name="finish",
    )(core, *parts)


AXES = ("ka", "aux")


def moved(x, points, parts, source):
    route = []
    for k in range(points):
        for a in range(parts):
            k2, a2 = source(k, a)
            route.append((k2 * parts + a2, k * parts + a))
    return lax.ppermute(x, AXES, route)


def pass_kernel(x, done, out):
    pass


def after(x, done):
    return pl.pallas_call(
        pass_kernel,
        out_shape=jax.ShapeDtypeStruct(x.shape, x.dtype),
        in_specs=[ANY] * 2,
        out_specs=ANY,
        input_output_aliases={0: 0},
        compiler_params=params(1),
        cost_estimate=cost(0, 0),
        name="after",
    )(x, done)


def body(lambda_blocks, left_tiles, right_tiles):
    points, parts = lax.axis_size("ka"), lax.axis_size("aux")
    go = lambda x, source: moved(x, points, parts, source)
    near = lambda x: go(x, lambda k, a: ((k + 1) % points, a))
    far = lambda x: go(x, lambda k, a: ((k + points // 4) % points, a))
    zed = lambda x: go(x, lambda k, a: (k, a ^ 2))
    core = lambda x: go(x, lambda k, a: (k, a ^ 1))
    which = (lax.axis_index("aux") % 2).astype(jnp.int32).reshape(1)

    lam, again = flat_lambda(lambda_blocks.reshape(32, 64, 64))
    lam_z, far_own = zed(lam), far(lam)
    factors, done = {}, lam
    for s in (1, 0):
        done, sent = flat_factors(which, left_tiles[0], right_tiles[0], s, done)
        factors[s] = done, sent, core(sent)
    w_far = [build(0, *factors[1], done)]
    near_own = near(after(again, w_far[0]))
    w_far.append(build(HALF, *factors[1], w_far[0], 40000))
    lam_z, near_own, far_own = [after(x, w_far[1]) for x in (lam_z, near_own, far_own)]
    far_z, near_z = far(lam_z), near(lam_z)
    w_near = [build(0, *factors[0], near_own)]
    w_near.append(build(HALF, *factors[0], w_near[0]))
    far_z, near_z = after(far_z, w_near[1]), after(near_z, w_near[1])
    so_far = contract([far_own, core(far_own), far_z, core(far_z)], w_far)
    pieces = [near_own, core(near_own), near_z, core(near_z)]
    p_own, p_core, p_zed, p_diag = contract(pieces, w_near, so_far[0])
    out = finish(which, [p_own, zed(p_zed), core(p_core), zed(core(p_diag))])
    return out.reshape(lambda_blocks.shape)


def solution(mesh):
    placed = P("ka", None, "aux", None, None)
    return jax.shard_map(body, mesh=mesh, in_specs=(placed,) * 3, out_specs=placed, check_vma=False)
```

```python
import functools

import jax
import jax.numpy as jnp
from jax import lax
from jax.experimental import pallas as pl
from jax.experimental.pallas import tpu as pltpu
from jax.sharding import PartitionSpec as P

BF16 = jnp.bfloat16
F32 = jnp.float32
VMEM = pl.BlockSpec(memory_space=pltpu.VMEM)
SMEM = pl.BlockSpec(memory_space=pltpu.SMEM)
ANY = pl.BlockSpec(memory_space=pl.ANY)
MIB = 2**20


def params(mib, **kw):
    return pltpu.CompilerParams(vmem_limit_bytes=mib * MIB, **kw)


def spread(src, dst, held, count, swap, unroll):
    def put(n, _):
        x = src[n].T if swap else src[n]
        rows = pl.ds(pl.multiple_of(n * 32, 32), 32)
        held[rows, :] = jnp.concatenate([x[:32], x[32:]], axis=1).astype(F32)
        return 0

    lax.fori_loop(0, count, put, 0, unroll=unroll)
    for ref, first in dst:
        take(ref, held, first, count)


def take(dst, held, first, count):
    for t in range(dst.shape[1] // 128):
        dst[:, t * 128 : (t + 1) * 128] = held[pl.ds(first + t, count, stride=32), :].astype(BF16)


def in_hbm(x):
    return pltpu.with_memory_space_constraint(x, pltpu.HBM)


def in_vmem(x):
    return pltpu.with_memory_space_constraint(x, pltpu.VMEM)


def cost(flops, mib):
    return pl.CostEstimate(flops=flops // 1000, bytes_accessed=int(mib * 1024), transcendentals=0)


def lambda_kernel(lam, out, again, held):
    spread(lam, [(out, 0)], held, lam.shape[0], True, 32)
    again[...] = out[...]


def flat_lambda(lam):
    n = lam.shape[0]
    flat = pl.BlockSpec((n, 4096), lambda i: (0, 0))
    return pl.pallas_call(
        lambda_kernel,
        grid=(1,),
        out_shape=[jax.ShapeDtypeStruct((n, 4096), BF16)] * 2,
        in_specs=[pl.BlockSpec((n, 64, 64), lambda i: (0, 0, 0))],
        out_specs=[flat] * 2,
        scratch_shapes=[pltpu.VMEM((n * 32, 128), F32)],
        compiler_params=params(8),
        cost_estimate=cost(0, 6),
        name="flat_lambda",
    )(in_hbm(lam))


def factor_kernel(core, left, right, done, mine, sent, held_l, held_r):
    half = core[0]
    spread(left.at[0], [(mine, half * 16), (sent.at[:, :2048], (1 - half) * 16)], held_l, 32, False, 32)
    spread(right.at[0], [(sent.at[:, 2048:], 0)], held_r, 32, True, 32)


def flat_factors(core, left, right, s, done):
    block = pl.BlockSpec((1, 32, 64, 64), lambda i: (s, i, 0, 0))
    return pl.pallas_call(
        factor_kernel,
        grid=(2,),
        out_shape=[jax.ShapeDtypeStruct((64, n), BF16) for n in (2048, 6144)],
        in_specs=[SMEM, block, block, ANY],
        out_specs=[pl.BlockSpec((32, n), lambda i: (i, 0)) for n in (2048, 6144)],
        scratch_shapes=[pltpu.VMEM((32 * 32, 128), F32)] * 2,
        compiler_params=params(8),
        cost_estimate=cost(0, 400000),
        name="flat_factors",
    )(core, in_hbm(left), in_hbm(right), done)


TS = 8
HALF = 16


def build_kernel(first, mine, sent, got_here, done, w, x, s):
    for ap in range(16):
        at = slice(ap * 128, (ap + 1) * 128)
        v = jnp.concatenate([mine[:, at], got_here[:, at]], axis=0).T
        x[ap * 64 : (ap + 1) * 64, :] = jnp.concatenate([v[:64], v[64:]], axis=1)
    low = lax.broadcasted_iota(jnp.int32, (128, 128), 1) < 64
    zero = jnp.zeros((128, 128), BF16)

    def fill(slot, u):
        for i in range(TS):
            t = first + u * TS + i
            at = slice(2048 + t * 128, 2048 + (t + 1) * 128)
            v = jnp.concatenate([sent[:, at], got_here[:, at]], axis=0)
            r = jnp.concatenate([v[:, 64:], v[:, :64]], axis=1)
            a, b = i * 256, i * 256 + 128
            s[slot, 0:128, a : a + 128] = jnp.where(low, v, zero)
            s[slot, 0:128, b : b + 128] = jnp.where(low, r, zero)
            s[slot, 128:256, a : a + 128] = jnp.where(low, zero, r)
            s[slot, 128:256, b : b + 128] = jnp.where(low, zero, v)

    def work(u, slot):
        if u + 1 < HALF // TS:
            fill(1 - slot, u + 1)
        for n in range(TS // 2):
            for m in range(8):
                got = jnp.dot(
                    x[m * 128 : (m + 1) * 128, :],
                    s[slot, :, n * 512 : (n + 1) * 512],
                    preferred_element_type=F32,
                ).astype(BF16)
                for i in range(4):
                    row = (u * TS * 2 + n * 4 + i) * 64
                    for p in range(2):
                        w[row : row + 64, (m * 2 + p) * 128 : (m * 2 + p + 1) * 128] = got[
                            p * 64 : (p + 1) * 64, i * 128 : (i + 1) * 128
                        ]

    fill(0, 0)
    for u in range(HALF // TS):
        work(u, u % 2)


def build(first, mine, sent, got, done, weight=1):
    return pl.pallas_call(
        functools.partial(build_kernel, first),
        out_shape=pltpu.VMEM((HALF * 128, 2048), BF16),
        in_specs=[VMEM] * 3 + [ANY],
        out_specs=VMEM,
        scratch_shapes=[pltpu.VMEM((1024, 256), BF16), pltpu.VMEM((2, 256, 256 * TS), BF16)],
        compiler_params=params(6),
        cost_estimate=cost(2 * 1024 * 256 * 4096 * weight, 9 * weight),
        name="build_w",
    )(mine, sent, got, done)


def contract_kernel(last, first, *refs):
    n_out = 4 if last else 1
    pieces, ws, so_far, outs, (lhs, sems) = refs[:4], refs[4:6], refs[6:-2 - n_out], refs[-2 - n_out : -2], refs[-2:]
    copies = []
    for p, piece in enumerate(pieces):
        copies.append(pltpu.make_async_copy(piece, lhs.at[pl.ds(p * 32, 32)], sems.at[p]))
    for c in copies:
        c.start()
    for c in copies:
        c.wait()
    width = 512
    deep = HALF * 128
    for n in range(outs[0].shape[1] // width):
        at = slice(n * width, (n + 1) * width)
        src = slice(first + n * width, first + (n + 1) * width)
        got = jnp.dot(lhs[:, :deep], ws[0][:, src], preferred_element_type=F32)
        got += jnp.dot(lhs[:, deep:], ws[1][:, src], preferred_element_type=F32)
        if last:
            got += so_far[0][:, src]
            own, core, zed, diag = outs
            own[:, at] = got[0:32]
            core[:, at] = got[32:64]
            zed[:, at] = got[64:96].astype(BF16)
            diag[:, at] = got[96:128].astype(BF16)
        else:
            outs[0][:, at] = got


def contract(pieces, ws, so_far=None, first=0, cols=2048):
    last = so_far is not None
    rows = ((32, F32), (32, F32), (32, BF16), (32, BF16)) if last else ((128, F32),)
    return pl.pallas_call(
        functools.partial(contract_kernel, last, first),
        out_shape=[jax.ShapeDtypeStruct((r, cols), t) for r, t in rows],
        in_specs=[ANY] * 4 + [VMEM] * (2 + last),
        out_specs=[VMEM] * len(rows),
        scratch_shapes=[pltpu.VMEM((128, 4096), BF16), pltpu.SemaphoreType.DMA((4,))],
        compiler_params=params(8),
        cost_estimate=cost(2 * 128 * 4096 * 2048, 12),
        name="contract",
    )(*pieces, *(in_vmem(w) for w in ws), *((so_far,) if last else ()))


def finish_kernel(core, *refs):
    parts, out, held = refs[:-2], refs[-2], refs[-1]
    half = core[0]
    per = 16
    for ap in range(16):
        own, zed, other, diag = parts[ap // per * 4 : ap // per * 4 + 4]
        at = slice(ap % per * 128, (ap % per + 1) * 128)
        held[pl.ds(half * 16 + ap, 32, stride=32), :] = own[:, at] + zed[:, at].astype(F32)
        held[pl.ds((1 - half) * 16 + ap, 32, stride=32), :] = other[:, at] + diag[:, at].astype(F32)

    def put(n, _):
        x = held[pl.ds(pl.multiple_of(n * 32, 32), 32), :]
        out[n, 0:32, :] = x[:, :64]
        out[n, 32:64, :] = x[:, 64:]
        return 0

    lax.fori_loop(0, 32, put, 0, unroll=16)


def finish(core, parts):
    return pl.pallas_call(
        finish_kernel,
        out_shape=jax.ShapeDtypeStruct((32, 64, 64), F32),
        in_specs=[SMEM] + [VMEM] * len(parts),
        out_specs=VMEM,
        scratch_shapes=[pltpu.VMEM((1024, 128), F32)],
        compiler_params=params(8),
        cost_estimate=cost(0, 6),
        name="finish",
    )(core, *parts)


AXES = ("ka", "aux")


def moved(x, points, parts, source):
    route = []
    for k in range(points):
        for a in range(parts):
            k2, a2 = source(k, a)
            route.append((k2 * parts + a2, k * parts + a))
    return lax.ppermute(x, AXES, route)


def pass_kernel(x, done, out):
    pass


def after(x, done):
    return pl.pallas_call(
        pass_kernel,
        out_shape=jax.ShapeDtypeStruct(x.shape, x.dtype),
        in_specs=[ANY] * 2,
        out_specs=ANY,
        input_output_aliases={0: 0},
        compiler_params=params(1),
        cost_estimate=cost(0, 0),
        name="after",
    )(x, done)


def body(lambda_blocks, left_tiles, right_tiles):
    points, parts = lax.axis_size("ka"), lax.axis_size("aux")
    go = lambda x, source: moved(x, points, parts, source)
    near = lambda x: go(x, lambda k, a: ((k + 1) % points, a))
    far = lambda x: go(x, lambda k, a: ((k + points // 4) % points, a))
    zed = lambda x: go(x, lambda k, a: (k, a ^ 2))
    core = lambda x: go(x, lambda k, a: (k, a ^ 1))
    which = (lax.axis_index("aux") % 2).astype(jnp.int32).reshape(1)

    lam, again = flat_lambda(lambda_blocks.reshape(32, 64, 64))
    lam_z, far_own = zed(lam), far(lam)
    factors, done = {}, lam
    for s in (1, 0):
        done, sent = flat_factors(which, left_tiles[0], right_tiles[0], s, done)
        factors[s] = done, sent, core(sent)
    w_far = [build(0, *factors[1], done)]
    near_own = near(after(again, w_far[0]))
    w_far.append(build(HALF, *factors[1], w_far[0], 40000))
    lam_z, far_own = after(lam_z, w_far[1]), after(far_own, w_far[1])
    far_z, near_z = far(lam_z), near(lam_z)
    w_near = [build(0, *factors[0], lam_z)]
    near_own = after(near_own, w_near[0])
    w_near.append(build(HALF, *factors[0], near_own))
    far_z, near_z = after(far_z, w_near[1]), after(near_z, w_near[1])
    so_far = contract([far_own, core(far_own), far_z, core(far_z)], w_far)
    pieces = [near_own, core(near_own), near_z, core(near_z)]
    p_own, p_core, p_zed, p_diag = contract(pieces, w_near, so_far[0])
    out = finish(which, [p_own, zed(p_zed), core(p_core), zed(core(p_diag))])
    return out.reshape(lambda_blocks.shape)


def solution(mesh):
    placed = P("ka", None, "aux", None, None)
    return jax.shard_map(body, mesh=mesh, in_specs=(placed,) * 3, out_specs=placed, check_vma=False)
```

```python
import functools

import jax
import jax.numpy as jnp
from jax import lax
from jax.experimental import pallas as pl
from jax.experimental.pallas import tpu as pltpu
from jax.sharding import PartitionSpec as P

BF16 = jnp.bfloat16
F32 = jnp.float32
VMEM = pl.BlockSpec(memory_space=pltpu.VMEM)
SMEM = pl.BlockSpec(memory_space=pltpu.SMEM)
ANY = pl.BlockSpec(memory_space=pl.ANY)
MIB = 2**20


def params(mib, **kw):
    return pltpu.CompilerParams(vmem_limit_bytes=mib * MIB, **kw)


def spread(src, dst, held, count, swap, unroll):
    def put(n, _):
        x = src[n].T if swap else src[n]
        rows = pl.ds(pl.multiple_of(n * 32, 32), 32)
        held[rows, :] = jnp.concatenate([x[:32], x[32:]], axis=1).astype(F32)
        return 0

    lax.fori_loop(0, count, put, 0, unroll=unroll)
    for ref, first in dst:
        take(ref, held, first, count)


def take(dst, held, first, count):
    for t in range(dst.shape[1] // 128):
        dst[:, t * 128 : (t + 1) * 128] = held[pl.ds(first + t, count, stride=32), :].astype(BF16)


def in_hbm(x):
    return pltpu.with_memory_space_constraint(x, pltpu.HBM)


def in_vmem(x):
    return pltpu.with_memory_space_constraint(x, pltpu.VMEM)


def cost(flops, mib):
    return pl.CostEstimate(flops=flops // 1000, bytes_accessed=int(mib * 1024), transcendentals=0)


def lambda_kernel(lam, out, again, held):
    spread(lam, [(out, 0)], held, lam.shape[0], True, 32)
    again[...] = out[...]


def flat_lambda(lam):
    n = lam.shape[0]
    flat = pl.BlockSpec((n, 4096), lambda i: (0, 0))
    return pl.pallas_call(
        lambda_kernel,
        grid=(1,),
        out_shape=[jax.ShapeDtypeStruct((n, 4096), BF16)] * 2,
        in_specs=[pl.BlockSpec((n, 64, 64), lambda i: (0, 0, 0))],
        out_specs=[flat] * 2,
        scratch_shapes=[pltpu.VMEM((n * 32, 128), F32)],
        compiler_params=params(8),
        cost_estimate=cost(0, 6),
        name="flat_lambda",
    )(in_hbm(lam))


def factor_kernel(core, left, right, done, mine, sent, held_l, held_r):
    half = core[0]
    spread(left.at[0], [(mine, half * 16), (sent.at[:, :2048], (1 - half) * 16)], held_l, 32, False, 32)
    spread(right.at[0], [(sent.at[:, 2048:], 0)], held_r, 32, True, 32)


def flat_factors(core, left, right, s, done):
    block = pl.BlockSpec((1, 32, 64, 64), lambda i: (s, i, 0, 0))
    return pl.pallas_call(
        factor_kernel,
        grid=(2,),
        out_shape=[jax.ShapeDtypeStruct((64, n), BF16) for n in (2048, 6144)],
        in_specs=[SMEM, block, block, ANY],
        out_specs=[pl.BlockSpec((32, n), lambda i: (i, 0)) for n in (2048, 6144)],
        scratch_shapes=[pltpu.VMEM((32 * 32, 128), F32)] * 2,
        compiler_params=params(8),
        cost_estimate=cost(0, 400000),
        name="flat_factors",
    )(core, in_hbm(left), in_hbm(right), done)


TS = 8
HALF = 16


def build_kernel(first, mine, sent, got_here, done, w, x, s):
    for ap in range(16):
        at = slice(ap * 128, (ap + 1) * 128)
        v = jnp.concatenate([mine[:, at], got_here[:, at]], axis=0).T
        x[ap * 64 : (ap + 1) * 64, :] = jnp.concatenate([v[:64], v[64:]], axis=1)
    low = lax.broadcasted_iota(jnp.int32, (128, 128), 1) < 64
    zero = jnp.zeros((128, 128), BF16)

    def fill(slot, u):
        for i in range(TS):
            t = first + u * TS + i
            at = slice(2048 + t * 128, 2048 + (t + 1) * 128)
            v = jnp.concatenate([sent[:, at], got_here[:, at]], axis=0)
            r = jnp.concatenate([v[:, 64:], v[:, :64]], axis=1)
            a, b = i * 256, i * 256 + 128
            s[slot, 0:128, a : a + 128] = jnp.where(low, v, zero)
            s[slot, 0:128, b : b + 128] = jnp.where(low, r, zero)
            s[slot, 128:256, a : a + 128] = jnp.where(low, zero, r)
            s[slot, 128:256, b : b + 128] = jnp.where(low, zero, v)

    def work(u, slot):
        if u + 1 < HALF // TS:
            fill(1 - slot, u + 1)
        for n in range(TS // 2):
            for m in range(8):
                got = jnp.dot(
                    x[m * 128 : (m + 1) * 128, :],
                    s[slot, :, n * 512 : (n + 1) * 512],
                    preferred_element_type=F32,
                ).astype(BF16)
                for i in range(4):
                    row = (u * TS * 2 + n * 4 + i) * 64
                    for p in range(2):
                        w[row : row + 64, (m * 2 + p) * 128 : (m * 2 + p + 1) * 128] = got[
                            p * 64 : (p + 1) * 64, i * 128 : (i + 1) * 128
                        ]

    fill(0, 0)
    for u in range(HALF // TS):
        work(u, u % 2)


def build(first, mine, sent, got, done, weight=1):
    return pl.pallas_call(
        functools.partial(build_kernel, first),
        out_shape=pltpu.VMEM((HALF * 128, 2048), BF16),
        in_specs=[VMEM] * 3 + [ANY],
        out_specs=VMEM,
        scratch_shapes=[pltpu.VMEM((1024, 256), BF16), pltpu.VMEM((2, 256, 256 * TS), BF16)],
        compiler_params=params(6),
        cost_estimate=cost(2 * 1024 * 256 * 4096 * weight, 9 * weight),
        name="build_w",
    )(mine, sent, got, done)


def contract_kernel(last, first, *refs):
    n_out = 4 if last else 1
    pieces, ws, so_far, outs, (lhs, sems) = refs[:4], refs[4:6], refs[6:-2 - n_out], refs[-2 - n_out : -2], refs[-2:]
    copies = []
    for p, piece in enumerate(pieces):
        copies.append(pltpu.make_async_copy(piece, lhs.at[pl.ds(p * 32, 32)], sems.at[p]))
    for c in copies:
        c.start()
    for c in copies:
        c.wait()
    width = 512
    deep = HALF * 128
    for n in range(outs[0].shape[1] // width):
        at = slice(n * width, (n + 1) * width)
        src = slice(first + n * width, first + (n + 1) * width)
        got = jnp.dot(lhs[:, :deep], ws[0][:, src], preferred_element_type=F32)
        got += jnp.dot(lhs[:, deep:], ws[1][:, src], preferred_element_type=F32)
        if last:
            got += so_far[0][:, src]
            own, core, zed, diag = outs
            own[:, at] = got[0:32]
            core[:, at] = got[32:64]
            zed[:, at] = got[64:96].astype(BF16)
            diag[:, at] = got[96:128].astype(BF16)
        else:
            outs[0][:, at] = got


def contract(pieces, ws, so_far=None, first=0, cols=2048):
    last = so_far is not None
    rows = ((32, F32), (32, F32), (32, BF16), (32, BF16)) if last else ((128, F32),)
    return pl.pallas_call(
        functools.partial(contract_kernel, last, first),
        out_shape=[jax.ShapeDtypeStruct((r, cols), t) for r, t in rows],
        in_specs=[ANY] * 4 + [VMEM] * (2 + last),
        out_specs=[VMEM] * len(rows),
        scratch_shapes=[pltpu.VMEM((128, 4096), BF16), pltpu.SemaphoreType.DMA((4,))],
        compiler_params=params(8),
        cost_estimate=cost(2 * 128 * 4096 * 2048, 12),
        name="contract",
    )(*pieces, *(in_vmem(w) for w in ws), *((so_far,) if last else ()))


def finish_kernel(core, *refs):
    parts, out, held = refs[:-2], refs[-2], refs[-1]
    half = core[0]
    own, zed, other, diag = parts
    rows = pl.ds(pl.multiple_of(pl.program_id(0) * 16, 16), 16)
    for ap in range(16):
        at = slice(ap * 128, (ap + 1) * 128)
        held[pl.ds(half * 16 + ap, 16, stride=32), :] = own[rows, at] + zed[rows, at].astype(F32)
        held[pl.ds((1 - half) * 16 + ap, 16, stride=32), :] = other[rows, at] + diag[rows, at].astype(F32)
    for n in range(16):
        x = held[n * 32 : (n + 1) * 32, :]
        out[n, 0:32, :] = x[:, :64]
        out[n, 32:64, :] = x[:, 64:]


def finish(core, parts):
    return pl.pallas_call(
        finish_kernel,
        grid=(2,),
        out_shape=jax.ShapeDtypeStruct((32, 64, 64), F32),
        in_specs=[SMEM] + [VMEM] * len(parts),
        out_specs=pl.BlockSpec((16, 64, 64), lambda i: (i, 0, 0)),
        scratch_shapes=[pltpu.VMEM((512, 128), F32)],
        compiler_params=params(8),
        cost_estimate=cost(0, 6),
        name="finish",
    )(core, *parts)


AXES = ("ka", "aux")


def moved(x, points, parts, source):
    route = []
    for k in range(points):
        for a in range(parts):
            k2, a2 = source(k, a)
            route.append((k2 * parts + a2, k * parts + a))
    return lax.ppermute(x, AXES, route)


def pass_kernel(x, done, out):
    pass


def after(x, done):
    return pl.pallas_call(
        pass_kernel,
        out_shape=jax.ShapeDtypeStruct(x.shape, x.dtype),
        in_specs=[ANY] * 2,
        out_specs=ANY,
        input_output_aliases={0: 0},
        compiler_params=params(1),
        cost_estimate=cost(0, 0),
        name="after",
    )(x, done)


def body(lambda_blocks, left_tiles, right_tiles):
    points, parts = lax.axis_size("ka"), lax.axis_size("aux")
    go = lambda x, source: moved(x, points, parts, source)
    near = lambda x: go(x, lambda k, a: ((k + 1) % points, a))
    far = lambda x: go(x, lambda k, a: ((k + points // 4) % points, a))
    zed = lambda x: go(x, lambda k, a: (k, a ^ 2))
    core = lambda x: go(x, lambda k, a: (k, a ^ 1))
    which = (lax.axis_index("aux") % 2).astype(jnp.int32).reshape(1)

    lam, again = flat_lambda(lambda_blocks.reshape(32, 64, 64))
    lam_z, far_own = zed(lam), far(lam)
    factors, done = {}, lam
    for s in (1, 0):
        done, sent = flat_factors(which, left_tiles[0], right_tiles[0], s, done)
        factors[s] = done, sent, core(sent)
    w_far = [build(0, *factors[1], done)]
    near_own = near(after(again, w_far[0]))
    w_far.append(build(HALF, *factors[1], w_far[0], 40000))
    lam_z, far_own = after(lam_z, w_far[1]), after(far_own, w_far[1])
    far_z, near_z = far(lam_z), near(lam_z)
    w_near = [build(0, *factors[0], lam_z)]
    near_own = after(near_own, w_near[0])
    w_near.append(build(HALF, *factors[0], near_own))
    far_z, near_z = after(far_z, w_near[1]), after(near_z, w_near[1])
    so_far = contract([far_own, core(far_own), far_z, core(far_z)], w_far)
    pieces = [near_own, core(near_own), near_z, core(near_z)]
    p_own, p_core, p_zed, p_diag = contract(pieces, w_near, so_far[0])
    out = finish(which, [p_own, zed(p_zed), core(p_core), zed(core(p_diag))])
    return out.reshape(lambda_blocks.shape)


def solution(mesh):
    placed = P("ka", None, "aux", None, None)
    return jax.shard_map(body, mesh=mesh, in_specs=(placed,) * 3, out_specs=placed, check_vma=False)
```
